256 devices in a mesh: ctx: 32 (over y, z), head: 8 (over x, core).
Axes of the slice: x: 4, y: 4, z: 8, core: 2. Of those that a mesh axis runs over, the one named last changes fastest.
Arguments:
- queries: bfloat16 [24576, 1024], P('ctx', 'head'), may hold values from -4.5 to 4.5
- keys_values: bfloat16 [2, 24576, 1024], P(None, 'ctx', 'head'), may hold values from -4.5 to 4.5
- out_weight: bfloat16 [1024, 6144], P(None, 'head'), may hold values from -0.1875 to 0.1875
- group_owner: int32 [64], replicated, may hold values from 0 to 63, each once
- clip_ids: int32 [64], replicated, may hold values from 0 to 2, as said below
- mask_types: int32 [3], replicated, may hold values from 0 to 1
Outputs:
- mixed: bfloat16 [24576, 6144], P('ctx', 'head')
The draws below stay inside these ranges and needn't reach their ends.
Inputs may be any that keep to these rules, and one draw needn't show every extreme that they name: `group_owner`: each group position appears once; group slot s is stored on ctx index s // 2. `clip_ids`: never falls along positions; each clip holds 1 to 32 consecutive positions and one holds exactly 32. `mask_types`: 0: a group sees the groups of its clip up to itself; 1: all groups of its clip.
All inputs are finite; a program needn't handle non-finite values.
Results may differ from the reference program's by a relative error of at most 0.011.
Values may be sent and summed in bfloat16 or wider, within the bound.
No kernel may reach another device: no remote copies, remote signals or barrier semaphores. Data moves between devices by JAX's collectives and lax.ppermute only.
A program may use at most 64 MiB of HBM per device.

```python
import math
import jax
import jax.numpy as jnp
from jax import lax

D = 6144
HEAD_DIM = 128
HEADS = 8
GROUP = 384
GROUPS_DEV = 2
NCLIP = 3
TOK_DEV = 768
NGR = 64
MAXCLIP = 32
TOKENS = 24576
N_CTX = 32


def draw_queries(key, part):
    key = jax.random.fold_in(key, 11)
    shape = (TOKENS, HEADS * HEAD_DIM)
    values = jax.random.truncated_normal(key, -4.5, 4.5, shape, jnp.float32)
    return values.astype(jnp.bfloat16)


def draw_keys_values(key, part):
    key = jax.random.fold_in(key, 12)
    shape = (TOKENS, HEADS * HEAD_DIM)
    value_part = jax.random.truncated_normal(jax.random.fold_in(key, 2), -4.5, 4.5, shape, jnp.float32)
    key_part = jax.random.truncated_normal(key, -4.5, 4.5, shape, jnp.float32)
    return jnp.stack([key_part, value_part]).astype(jnp.bfloat16)


def draw_clip_ids(key, part):
    key = jax.random.fold_in(key, 21)
    remain = NGR - MAXCLIP
    cut_key = jax.random.fold_in(key, 1)
    big_key = jax.random.fold_in(key, 2)
    order = jax.random.permutation(cut_key, remain - 1).astype(jnp.int32)
    cuts = jnp.sort(order[:NCLIP - 2] + 1)
    bounds = jnp.concatenate([jnp.zeros((1,), jnp.int32), cuts, jnp.full((1,), remain, jnp.int32)])
    others = bounds[1:] - bounds[:-1]
    big_clip = jax.random.randint(big_key, (), 0, NCLIP, jnp.int32)
    index = jnp.arange(NCLIP, dtype=jnp.int32)
    other_index = jnp.clip(index - (index > big_clip).astype(jnp.int32), 0, NCLIP - 2)
    lengths = jnp.where(index == big_clip, MAXCLIP, others[other_index]).astype(jnp.int32)
    ends = jnp.cumsum(lengths).astype(jnp.int32)
    places = jnp.arange(NGR, dtype=jnp.int32)
    return jnp.sum((places[:, None] >= ends[None, :]).astype(jnp.int32), axis=1).astype(jnp.int32)


def level_of(own_key, extent, shards, least, top_value):
    def one(position, blocks):
        steps = jax.random.uniform(jax.random.fold_in(jax.random.fold_in(own_key, 6), position), (blocks,), jnp.float32, least / len(shards), top_value / len(shards))
        return jnp.repeat(jnp.exp(steps), extent[position] // blocks).reshape((-1,) + (1,) * (len(extent) - position - 1))

    level = one(*shards[0])
    for cut in shards[1:]:
        level = level * one(*cut)
    return level


def gaussian(key, shape, spread, bound, cuts=(), kind=jnp.bfloat16):
    values = jax.random.normal(key, shape, jnp.float32) * spread
    if len(cuts) > 0:
        values = level_of(key, shape, cuts, -0.22, 0.18) * values
    return jnp.clip(values, min=-bound, max=bound).astype(kind)


def setup_inputs(seed: int = 0) -> dict:
    key_of = jax.random.split(jax.random.key(seed), 7)
    return {
        "queries": draw_queries(jax.random.fold_in(key_of[6], 71), 0),
        "keys_values": draw_keys_values(jax.random.fold_in(key_of[6], 71), 0),
        "out_weight": gaussian(key_of[2], (HEADS * HEAD_DIM, D), (HEADS * HEAD_DIM) ** -0.5, 0.1875, ((1, 8),)),
        "group_owner": jax.random.permutation(key_of[3], NGR).astype(jnp.int32),
        "clip_ids": draw_clip_ids(jax.random.fold_in(key_of[6], 71), 0),
        "mask_types": jax.random.randint(key_of[5], (NCLIP,), 0, 2).astype(jnp.int32),
    }


def reference(queries, keys_values, out_weight, group_owner, clip_ids, mask_types):
    clip_of = clip_ids[group_owner]
    kind_of = mask_types[clip_of]
    key_pos = jnp.repeat(group_owner, GROUP)
    key_clip = jnp.repeat(clip_of, GROUP)
    score_scale = 1.0 / math.sqrt(HEAD_DIM)
    key_heads = keys_values[0].astype(jnp.float32).reshape(TOKENS, HEADS, HEAD_DIM).transpose(1, 0, 2)
    value_heads = keys_values[1].astype(jnp.float32).reshape(TOKENS, HEADS, HEAD_DIM).transpose(1, 0, 2)

    def one_rank(rank_index):
        query_rows = lax.dynamic_slice_in_dim(queries, rank_index * TOK_DEV, TOK_DEV, 0)
        query_rows = query_rows.astype(jnp.float32).reshape(TOK_DEV, HEADS, HEAD_DIM).transpose(1, 0, 2)
        group_start = (rank_index * GROUPS_DEV).astype(jnp.int32)
        own_pos = jnp.repeat(lax.dynamic_slice_in_dim(group_owner, group_start, GROUPS_DEV, 0), GROUP)
        own_clip = jnp.repeat(lax.dynamic_slice_in_dim(clip_of, group_start, GROUPS_DEV, 0), GROUP)
        own_kind = jnp.repeat(lax.dynamic_slice_in_dim(kind_of, group_start, GROUPS_DEV, 0), GROUP)
        token_seen = (own_clip[:, None] == key_clip[None, :]) & ((own_kind[:, None] == 1) | (key_pos[None, :] <= own_pos[:, None]))

        def one_head(operands):
            query_head, key_head, value_head = operands
            scores = jnp.dot(query_head, key_head.T) * score_scale
            scores = jnp.where(token_seen, scores, -jnp.inf)
            row_max = lax.optimization_barrier(jnp.max(scores, axis=1, keepdims=True))
            weights = jnp.exp(scores - row_max)
            totals = lax.optimization_barrier(jnp.sum(weights, axis=1))
            rounded = lax.optimization_barrier(weights.astype(jnp.bfloat16)).astype(jnp.float32)
            summed = jnp.dot(rounded, value_head)
            return summed / totals[:, None]
        result = lax.map(one_head, (query_rows, key_heads, value_heads))
        return result.transpose(1, 0, 2).reshape(TOK_DEV, HEADS * HEAD_DIM).astype(jnp.bfloat16)
    attended = lax.map(one_rank, jnp.arange(N_CTX, dtype=jnp.int32)).reshape(TOKENS, HEADS * HEAD_DIM)
    return jnp.dot(attended, out_weight, preferred_element_type=jnp.float32).astype(jnp.bfloat16)
```

```python
import functools
import math

import jax
import jax.numpy as jnp
from jax import lax
from jax.experimental import pallas as pl
from jax.experimental.pallas import tpu as pltpu
from jax.sharding import PartitionSpec as P

HEAD_DIM = 128
GROUP = 384
PER_RANK = 2
NY, NZ = 4, 8
NX, NCORE = 4, 2
NQ = NY * PER_RANK
TRASH = NQ
STAT_ROWS = 16
LOG2_SCALE = math.log2(math.e) / math.sqrt(HEAD_DIM)
LOWEST = -1e30
UNROLL = 2
F32, BF16 = jnp.float32, jnp.bfloat16

SMEM = pl.BlockSpec(memory_space=pltpu.SMEM)
VMEM = pl.BlockSpec(memory_space=pltpu.VMEM)
PARAMS = pltpu.CompilerParams(vmem_limit_bytes=40 << 20)


def along_y(step):
    return [(y * NZ + z, (y + step) % NY * NZ + z) for y in range(NY) for z in range(NZ)]


def along_z(step):
    return [(y * NZ + z, y * NZ + (z + step) % NZ) for y in range(NY) for z in range(NZ)]


def along_x(step):
    return [(x * NCORE + c, (x + step) % NX * NCORE + c) for x in range(NX) for c in range(NCORE)]


def other_core():
    return [(x * NCORE + c, x * NCORE + 1 - c) for x in range(NX) for c in range(NCORE)]


def list_pairs(offsets, rank, owner, clips, kinds, list_q, list_acc, list_k):
    my_y, my_z = rank // NZ, rank % NZ
    query = []
    for i in range(NQ):
        slot = ((my_y + i // PER_RANK) % NY * NZ + my_z) * PER_RANK + i % PER_RANK
        pos = owner[slot]
        clip = clips[pos]
        query.append((pos, clip, kinds[clip]))
    count = jnp.int32(0)
    for j, offset in enumerate(offsets):
        for g in range(PER_RANK):
            slot = (my_y * NZ + (my_z + offset) % NZ) * PER_RANK + g
            pos = owner[slot]
            clip = clips[pos]
            for i in range(NQ):
                q_pos, q_clip, q_kind = query[i]
                seen = (q_clip == clip) & ((q_kind == 1) | (pos <= q_pos))
                list_q[count] = i
                list_acc[count] = i
                list_k[count] = j * PER_RANK + g
                count = count + seen.astype(jnp.int32)
    for e in range(UNROLL + 1):
        list_q[count + e] = 0
        list_acc[count + e] = TRASH
        list_k[count + e] = 0
    return count


def attend(offsets, key_parts, first, last, *refs):
    refs = list(refs)
    rank_ref, owner, clips, kinds = refs[:4]
    del refs[:4]
    q_refs = refs[:NY]
    del refs[:NY]
    n_blocks = len(offsets)
    block_refs = refs[: sum(key_parts)]
    del refs[: sum(key_parts)]
    if not first:
        acc_in, max_in, sum_in = refs[:3]
        del refs[:3]
    if last:
        out_refs = refs[:NY]
        del refs[:NY]
    else:
        acc, run_max, run_sum = refs[:3]
        del refs[:3]
    qt, keys, vals, scores, list_q, list_acc, list_k = refs[:7]
    del refs[:7]
    if last:
        acc, run_max, run_sum = refs

    count = list_pairs(offsets, rank_ref[0], owner, clips, kinds, list_q, list_acc, list_k)

    for b in range(NY):
        for g in range(PER_RANK):
            qt[b * PER_RANK + g] = q_refs[b][g]
    at = 0
    for j in range(n_blocks):
        if key_parts[j] == 1:
            key_block, value_block = block_refs[at].at[0], block_refs[at].at[1]
        else:
            key_block, value_block = block_refs[at], block_refs[at + 1]
        at += key_parts[j]
        for g in range(PER_RANK):
            rows = pl.ds(g * GROUP, GROUP)
            keys[j * PER_RANK + g] = key_block[rows, :]
            vals[j * PER_RANK + g] = value_block[rows, :].T
    if first:
        acc[...] = jnp.zeros(acc.shape, F32)
        run_max[...] = jnp.full(run_max.shape, LOWEST, F32)
        run_sum[...] = jnp.zeros(run_sum.shape, F32)
    else:
        acc[...] = acc_in[...]
        run_max[...] = max_in[...]
        run_sum[...] = sum_in[...]

    def score(t):
        return jnp.dot(keys[list_k[t]], qt[list_q[t]], preferred_element_type=F32)

    scores[0] = score(0)

    def one_pair(t, slot):
        scores[(slot + 1) % 2] = score(t + 1)
        i = list_acc[t]
        tile = scores[slot % 2]
        old_max = run_max[i][:1]
        new_max = jnp.maximum(old_max, jnp.max(tile, axis=0, keepdims=True) * LOG2_SCALE)
        shrink = jnp.exp2(old_max - new_max)
        weights = jnp.exp2(tile * LOG2_SCALE - new_max)
        run_sum[i] = run_sum[i] * shrink + jnp.sum(weights.reshape(GROUP // 8, 8, GROUP), axis=0)
        acc[i] = acc[i] * shrink + jnp.dot(
            vals[list_k[t]], weights.astype(BF16), preferred_element_type=F32
        )
        run_max[i] = jnp.broadcast_to(new_max, (8, GROUP))

    def some_pairs(t, carry):
        for u in range(UNROLL):
            one_pair(UNROLL * t + u, u)
        return carry

    lax.fori_loop(0, (count + UNROLL - 1) // UNROLL, some_pairs, 0)

    if last:
        row = lax.broadcasted_iota(jnp.int32, (STAT_ROWS, GROUP), 0)
        for i in range(NQ):
            total = jnp.sum(run_sum[i], axis=0, keepdims=True)
            some = total > 0
            total = jnp.where(some, total, 1.0)
            level = jnp.where(some, run_max[i][:1] + jnp.log2(total), LOWEST)
            high = level.astype(BF16).astype(F32)
            middle = (level - high).astype(BF16).astype(F32)
            low = level - high - middle
            stats = jnp.where(row == 0, high, jnp.where(row == 1, middle, jnp.where(row == 2, low, 0.0)))
            out = out_refs[i // PER_RANK]
            g = i % PER_RANK
            out[g, :HEAD_DIM, :] = (acc[i] / total).astype(BF16)
            out[g, HEAD_DIM:, :] = stats.astype(BF16)


def attend_call(offsets, scalars, queries, blocks, state, last):
    first = state is None
    n_keys = len(offsets) * PER_RANK
    key_parts = tuple(len(b) for b in blocks)
    state_shapes = [
        (NQ + 1, HEAD_DIM, GROUP),
        (NQ + 1, 8, GROUP),
        (NQ + 1, 8, GROUP),
    ]
    operands = list(scalars) + list(queries) + [a for b in blocks for a in b] + list(state or ())
    if last:
        out_shape = [jax.ShapeDtypeStruct((PER_RANK, HEAD_DIM + STAT_ROWS, GROUP), BF16)] * NY
    else:
        out_shape = [jax.ShapeDtypeStruct(s, F32) for s in state_shapes]
    pairs = NQ * n_keys
    list_len = pairs + 2 * UNROLL + 2
    scratch = [
        pltpu.VMEM((NQ, HEAD_DIM, GROUP), BF16),
        pltpu.VMEM((n_keys, GROUP, HEAD_DIM), BF16),
        pltpu.VMEM((n_keys, HEAD_DIM, GROUP), BF16),
        pltpu.VMEM((2, GROUP, GROUP), F32),
    ] + [pltpu.SMEM((list_len,), jnp.int32)] * 3
    if last:
        scratch += [pltpu.VMEM(s, F32) for s in state_shapes]
    return pl.pallas_call(
        functools.partial(attend, offsets, key_parts, first, last),
        name="attend_" + "_".join(str(o % NZ) for o in offsets),
        in_specs=[SMEM] * len(scalars) + [VMEM] * (len(operands) - len(scalars)),
        out_specs=[VMEM] * len(out_shape),
        out_shape=out_shape,
        scratch_shapes=scratch,
        compiler_params=PARAMS,
        cost_estimate=pl.CostEstimate(
            flops=pairs * GROUP * GROUP * HEAD_DIM * 4,
            bytes_accessed=4 << 20,
            transcendentals=pairs * GROUP * GROUP // 2,
        ),
    )(*operands)


def merge(*refs):
    *parts, out = refs
    for g in range(PER_RANK):
        levels = []
        for part in parts:
            stats = part[g, HEAD_DIM:, :].astype(F32)
            levels.append(stats[0:1] + stats[1:2] + stats[2:3])
        top = functools.reduce(jnp.maximum, levels)
        shares = [jnp.exp2(level - top) for level in levels]
        whole = functools.reduce(jnp.add, shares)
        total = functools.reduce(
            jnp.add,
            [part[g, :HEAD_DIM, :].astype(F32) * (share / whole) for part, share in zip(parts, shares)],
        )
        out[pl.ds(g * GROUP, GROUP), :] = total.T.astype(BF16)


def project(head_ref, *refs):
    *blocks, weight, out, rows = refs
    me = head_ref[0]
    my_x, my_core = me // NCORE, me % NCORE
    for n, block in enumerate(blocks):
        step, side = n // NCORE, n % NCORE
        head = (my_x + NX - step) % NX * NCORE + (my_core + side) % NCORE
        rows[:, pl.ds(pl.multiple_of(head * HEAD_DIM, HEAD_DIM), HEAD_DIM)] = block[...]
    out[...] = jnp.dot(rows[...], weight[...], preferred_element_type=F32).astype(BF16)


def shards(queries, keys_values, out_weight, group_owner, clip_ids, mask_types):
    tok_dev = queries.shape[0]
    rank = lax.axis_index("ctx").astype(jnp.int32).reshape(1)
    head = lax.axis_index("head").astype(jnp.int32).reshape(1)
    scalars = (rank, group_owner, clip_ids, mask_types)

    up, down = [], []
    right = left = keys_values
    for s in range(NZ // 2 - 1):
        right = lax.ppermute(right, "ctx", along_z(1))
        left = lax.ppermute(left, "ctx", along_z(-1))
        up.append(right)
        down.append(left)
    far_keys = lax.ppermute(right[0], "ctx", along_z(1))
    far_values = lax.ppermute(left[1], "ctx", along_z(-1))

    own_q = jnp.swapaxes(queries.reshape(PER_RANK, GROUP, HEAD_DIM), 1, 2)
    all_q = [own_q] + [lax.ppermute(own_q, "ctx", along_y(-d)) for d in range(1, NY)]

    state = attend_call((0, -1, 1), scalars, all_q, [(keys_values,), (up[0],), (down[0],)], None, False)
    state = attend_call((-2, 2), scalars, all_q, [(up[1],), (down[1],)], state, False)
    state = attend_call((-3, 3), scalars, all_q, [(up[2],), (down[2],)], state, False)
    parts = attend_call((4,), scalars, all_q, [(far_keys, far_values)], state, True)

    parts = [parts[0]] + [lax.ppermute(parts[d], "ctx", along_y(d)) for d in range(1, NY)]
    attended = pl.pallas_call(
        merge,
        name="merge",
        in_specs=[VMEM] * NY,
        out_specs=VMEM,
        out_shape=jax.ShapeDtypeStruct((tok_dev, HEAD_DIM), BF16),
        compiler_params=PARAMS,
    )(*parts)

    blocks = []
    for d in range(NX):
        block = attended if d == 0 else lax.ppermute(attended, "head", along_x(d))
        blocks += [block, lax.ppermute(block, "head", other_core())]
    return pl.pallas_call(
        project,
        name="project",
        in_specs=[SMEM] + [VMEM] * (len(blocks) + 1),
        out_specs=VMEM,
        out_shape=jax.ShapeDtypeStruct((tok_dev, out_weight.shape[1]), BF16),
        scratch_shapes=[pltpu.VMEM((tok_dev, len(blocks) * HEAD_DIM), BF16)],
        compiler_params=PARAMS,
    )(head, *blocks, out_weight)


def solution(mesh):
    placed = (P("ctx", "head"), P(None, "ctx", "head"), P(None, "head"), P(), P(), P())
    return jax.shard_map(
        shards, mesh=mesh, in_specs=placed, out_specs=P("ctx", "head"), check_vma=False
    )
```

```python
import functools
import math

import jax
import jax.numpy as jnp
from jax import lax
from jax.experimental import pallas as pl
from jax.experimental.pallas import tpu as pltpu
from jax.sharding import PartitionSpec as P

HEAD_DIM = 128
GROUP = 384
PER_RANK = 2
NY, NZ = 4, 8
NX, NCORE = 4, 2
NGR = NY * NZ * PER_RANK
NQ = NY * PER_RANK
TRASH = NQ
STAT_ROWS = 16
LOG2_SCALE = math.log2(math.e) / math.sqrt(HEAD_DIM)
LOWEST = -1e30
UNROLL = 2
F32, BF16 = jnp.float32, jnp.bfloat16

SMEM = pl.BlockSpec(memory_space=pltpu.SMEM)
VMEM = pl.BlockSpec(memory_space=pltpu.VMEM)
PARAMS = pltpu.CompilerParams(vmem_limit_bytes=40 << 20)


def along_y(step):
    return [(y * NZ + z, (y + step) % NY * NZ + z) for y in range(NY) for z in range(NZ)]


def along_z(step):
    return [(y * NZ + z, y * NZ + (z + step) % NZ) for y in range(NY) for z in range(NZ)]


def along_x(step):
    return [(x * NCORE + c, (x + step) % NX * NCORE + c) for x in range(NX) for c in range(NCORE)]


def other_core():
    return [(x * NCORE + c, x * NCORE + 1 - c) for x in range(NX) for c in range(NCORE)]


def list_pairs(offsets, info, list_q, list_acc, list_k):
    rank = info[0]
    my_y, my_z = rank // NZ, rank % NZ

    def of_slot(slot):
        pos = info[1 + slot]
        return pos, info[1 + NGR + pos]

    query = []
    for i in range(NQ):
        slot = ((my_y + i // PER_RANK) % NY * NZ + my_z) * PER_RANK + i % PER_RANK
        pos, clip = of_slot(slot)
        query.append((pos, clip, info[1 + 2 * NGR + clip]))
    count = jnp.int32(0)
    for j, offset in enumerate(offsets):
        for g in range(PER_RANK):
            slot = (my_y * NZ + (my_z + offset) % NZ) * PER_RANK + g
            pos, clip = of_slot(slot)
            for i in range(NQ):
                q_pos, q_clip, q_kind = query[i]
                seen = (q_clip == clip) & ((q_kind == 1) | (pos <= q_pos))
                list_q[count] = i
                list_acc[count] = i
                list_k[count] = j * PER_RANK + g
                count = count + seen.astype(jnp.int32)
    for e in range(UNROLL + 1):
        list_q[count + e] = 0
        list_acc[count + e] = TRASH
        list_k[count + e] = 0
    return count


def prepare(kv, query, keys, vals, turned):
    for g in range(PER_RANK):
        rows = pl.ds(g * GROUP, GROUP)
        turned[g] = query[rows, :].T
        keys[g] = kv[0, rows, :]
        vals[g] = kv[1, rows, :].T


def attend(offsets, key_parts, first, last, *refs):
    refs = list(refs)

    def take(n):
        taken = refs[:n]
        del refs[:n]
        return taken

    (info,) = take(1)
    q_refs = take(NY if first else 1)
    block_refs = take(sum(key_parts))
    if not first:
        acc_in, max_in, sum_in = take(3)
    if last:
        out_refs = take(NY)
    else:
        acc, run_max, run_sum = take(3)
    (qt,) = take(1) if first else q_refs
    keys, vals, scores, list_q, list_acc, list_k = take(6)
    if last:
        acc, run_max, run_sum = refs

    count = list_pairs(offsets, info, list_q, list_acc, list_k)

    if first:
        for b in range(NY):
            for g in range(PER_RANK):
                if b == 0:
                    qt[g] = q_refs[b][g]
                else:
                    qt[b * PER_RANK + g] = q_refs[b][pl.ds(g * GROUP, GROUP), :].T
    at = 0
    for j, parts in enumerate(key_parts):
        if parts == 1:
            key_block, value_block = block_refs[at].at[0], block_refs[at].at[1]
        else:
            key_block, value_block = block_refs[at], block_refs[at + 1]
        at += parts
        for g in range(PER_RANK):
            rows = pl.ds(g * GROUP, GROUP)
            if len(key_block.shape) == 3:
                keys[j * PER_RANK + g] = key_block[g]
                vals[j * PER_RANK + g] = value_block[g]
            else:
                keys[j * PER_RANK + g] = key_block[rows, :]
                vals[j * PER_RANK + g] = value_block[rows, :].T
    if first:
        acc[...] = jnp.zeros(acc.shape, F32)
        run_max[...] = jnp.full(run_max.shape, LOWEST, F32)
        run_sum[...] = jnp.zeros(run_sum.shape, F32)
    elif last:
        acc[...] = acc_in[...]
        run_max[...] = max_in[...]
        run_sum[...] = sum_in[...]

    def score(t):
        return jnp.dot(keys[list_k[t]], qt[list_q[t]], preferred_element_type=F32)

    scores[0] = score(0)

    def one_pair(t, slot):
        scores[(slot + 1) % 2] = score(t + 1)
        i = list_acc[t]
        tile = scores[slot % 2]
        old_max = run_max[i][:1]
        new_max = jnp.maximum(old_max, jnp.max(tile, axis=0, keepdims=True) * LOG2_SCALE)
        shrink = jnp.exp2(old_max - new_max)
        weights = jnp.exp2(tile * LOG2_SCALE - new_max)
        run_sum[i] = run_sum[i] * shrink + jnp.sum(weights.reshape(GROUP // 8, 8, GROUP), axis=0)
        acc[i] = acc[i] * shrink + jnp.dot(
            vals[list_k[t]], weights.astype(BF16), preferred_element_type=F32
        )
        run_max[i] = jnp.broadcast_to(new_max, (8, GROUP))

    def some_pairs(t, carry):
        for u in range(UNROLL):
            one_pair(UNROLL * t + u, u)
        return carry

    lax.fori_loop(0, (count + UNROLL - 1) // UNROLL, some_pairs, 0)

    if last:
        row = lax.broadcasted_iota(jnp.int32, (STAT_ROWS, GROUP), 0)
        for i in range(NQ):
            total = jnp.sum(run_sum[i], axis=0, keepdims=True)
            some = total > 0
            total = jnp.where(some, total, 1.0)
            level = jnp.where(some, run_max[i][:1] + jnp.log2(total), LOWEST)
            high = level.astype(BF16).astype(F32)
            middle = (level - high).astype(BF16).astype(F32)
            low = level - high - middle
            stats = jnp.where(row == 0, high, jnp.where(row == 1, middle, jnp.where(row == 2, low, 0.0)))
            out = out_refs[i // PER_RANK]
            g = i % PER_RANK
            out[g, :HEAD_DIM, :] = (acc[i] / total).astype(BF16)
            out[g, HEAD_DIM:, :] = stats.astype(BF16)


def attend_call(offsets, info, queries, blocks, state, last):
    first = state is None
    n_keys = len(offsets) * PER_RANK
    key_parts = tuple(len(b) for b in blocks)
    state_shapes = [(NQ + 1, HEAD_DIM, GROUP), (NQ + 1, 8, GROUP), (NQ + 1, 8, GROUP)]
    operands = [info] + list(queries) + [a for b in blocks for a in b] + list(state or ())
    if last:
        out_shape = [jax.ShapeDtypeStruct((PER_RANK, HEAD_DIM + STAT_ROWS, GROUP), BF16)] * NY
    else:
        out_shape = [jax.ShapeDtypeStruct(s, F32) for s in state_shapes]
    if first:
        out_shape += [jax.ShapeDtypeStruct((NQ, HEAD_DIM, GROUP), BF16)]
    pairs = NQ * n_keys
    list_len = pairs + 2 * UNROLL + 2
    scratch = [
        pltpu.VMEM((n_keys, GROUP, HEAD_DIM), BF16),
        pltpu.VMEM((n_keys, HEAD_DIM, GROUP), BF16),
        pltpu.VMEM((2, GROUP, GROUP), F32),
    ] + [pltpu.SMEM((list_len,), jnp.int32)] * 3
    if last:
        scratch += [pltpu.VMEM(s, F32) for s in state_shapes]
    return pl.pallas_call(
        functools.partial(attend, offsets, key_parts, first, last),
        name="attend_" + "_".join(str(o % NZ) for o in offsets),
        in_specs=[SMEM] + [VMEM] * (len(operands) - 1),
        out_specs=[VMEM] * len(out_shape),
        out_shape=out_shape,
        scratch_shapes=scratch,
        compiler_params=PARAMS,
        input_output_aliases={} if first or last else {len(operands) - 3 + i: i for i in range(3)},
        cost_estimate=pl.CostEstimate(
            flops=pairs * GROUP * GROUP * HEAD_DIM * 4,
            bytes_accessed=4 << 20,
            transcendentals=pairs * GROUP * GROUP // 2,
        ),
    )(*operands)


def merge(*refs):
    *parts, out = refs
    for g in range(PER_RANK):
        levels = []
        for part in parts:
            stats = part[g, HEAD_DIM:, :].astype(F32)
            levels.append(stats[0:1] + stats[1:2] + stats[2:3])
        top = functools.reduce(jnp.maximum, levels)
        shares = [jnp.exp2(level - top) for level in levels]
        whole = functools.reduce(jnp.add, shares)
        total = functools.reduce(
            jnp.add,
            [part[g, :HEAD_DIM, :].astype(F32) * (share / whole) for part, share in zip(parts, shares)],
        )
        out[pl.ds(g * GROUP, GROUP), :] = total.T.astype(BF16)


def project(head_ref, *refs):
    *blocks, weight, out, rows = refs
    me = head_ref[0]
    my_x, my_core = me // NCORE, me % NCORE
    for n, block in enumerate(blocks):
        step, side = n // NCORE, n % NCORE
        head = (my_x + NX - step) % NX * NCORE + (my_core + side) % NCORE
        rows[:, pl.ds(pl.multiple_of(head * HEAD_DIM, HEAD_DIM), HEAD_DIM)] = block[...]
    out[...] = jnp.dot(rows[...], weight[...], preferred_element_type=F32).astype(BF16)


def shards(queries, keys_values, out_weight, group_owner, clip_ids, mask_types):
    tok_dev = queries.shape[0]
    rank = lax.axis_index("ctx").astype(jnp.int32).reshape(1)
    head = lax.axis_index("head").astype(jnp.int32).reshape(1)

    def onward(right, left):
        return lax.ppermute(right, "ctx", along_z(1)), lax.ppermute(left, "ctx", along_z(-1))

    right, left = onward(keys_values, keys_values)
    all_q = [lax.ppermute(queries, "ctx", along_y(-d)) for d in range(1, NY)]
    info = jnp.concatenate([rank, group_owner, clip_ids, mask_types])
    *own, own_q = pl.pallas_call(
        prepare,
        name="prepare",
        in_specs=[VMEM] * 2,
        out_specs=[VMEM] * 3,
        out_shape=[
            jax.ShapeDtypeStruct((PER_RANK, GROUP, HEAD_DIM), BF16),
            jax.ShapeDtypeStruct((PER_RANK, HEAD_DIM, GROUP), BF16),
            jax.ShapeDtypeStruct((PER_RANK, HEAD_DIM, GROUP), BF16),
        ],
        compiler_params=pltpu.CompilerParams(vmem_limit_bytes=8 << 20),
    )(keys_values, queries)
    all_q = [own_q] + all_q
    right, left, all_q, info, own = lax.optimization_barrier((right, left, all_q, info, own))

    next_right, next_left = onward(right, left)
    *state, q_turned = attend_call((0, -1, 1), info, all_q, [own, (right,), (left,)], None, False)
    right, left, state = lax.optimization_barrier((next_right, next_left, state))

    next_right, next_left = onward(right, left)
    state = attend_call((-2, 2), info, [q_turned], [(right,), (left,)], state, False)
    right, left, state = lax.optimization_barrier((next_right, next_left, state))

    far = onward(right[0], left[1])
    state = attend_call((-3, 3), info, [q_turned], [(right,), (left,)], state, False)
    parts = attend_call((4,), info, [q_turned], [far], state, True)

    parts = [parts[0]] + [lax.ppermute(parts[d], "ctx", along_y(d)) for d in range(1, NY)]
    attended = pl.pallas_call(
        merge,
        name="merge",
        in_specs=[VMEM] * NY,
        out_specs=VMEM,
        out_shape=jax.ShapeDtypeStruct((tok_dev, HEAD_DIM), BF16),
        compiler_params=PARAMS,
    )(*parts)

    blocks = []
    for d in range(NX):
        block = attended if d == 0 else lax.ppermute(attended, "head", along_x(d))
        blocks += [block, lax.ppermute(block, "head", other_core())]
    return pl.pallas_call(
        project,
        name="project",
        in_specs=[SMEM] + [VMEM] * (len(blocks) + 1),
        out_specs=VMEM,
        out_shape=jax.ShapeDtypeStruct((tok_dev, out_weight.shape[1]), BF16),
        scratch_shapes=[pltpu.VMEM((tok_dev, len(blocks) * HEAD_DIM), BF16)],
        compiler_params=PARAMS,
    )(head, *blocks, out_weight)


def solution(mesh):
    placed = (P("ctx", "head"), P(None, "ctx", "head"), P(None, "head"), P(), P(), P())
    return jax.shard_map(
        shards, mesh=mesh, in_specs=placed, out_specs=P("ctx", "head"), check_vma=False
    )
```

```python
import functools
import math

import jax
import jax.numpy as jnp
from jax import lax
from jax.experimental import pallas as pl
from jax.experimental.pallas import tpu as pltpu
from jax.sharding import PartitionSpec as P

HEAD_DIM = 128
GROUP = 384
PER_RANK = 2
NY, NZ = 4, 8
NX, NCORE = 4, 2
NGR = NY * NZ * PER_RANK
NQ = NY * PER_RANK
TRASH = NQ
STAT_ROWS = 16
STAT_PIECES = 3
LOG2_SCALE = math.log2(math.e) / math.sqrt(HEAD_DIM)
LOWEST = -1e30
UNROLL = 3
AHEAD = 2
F32, BF16 = jnp.float32, jnp.bfloat16

SMEM = pl.BlockSpec(memory_space=pltpu.SMEM)
VMEM = pl.BlockSpec(memory_space=pltpu.VMEM)
PARAMS = pltpu.CompilerParams(vmem_limit_bytes=40 << 20)


def along_y(step):
    return [(y * NZ + z, (y + step) % NY * NZ + z) for y in range(NY) for z in range(NZ)]


def along_z(step):
    return [(y * NZ + z, y * NZ + (z + step) % NZ) for y in range(NY) for z in range(NZ)]


def along_x(step):
    return [(x * NCORE + c, (x + step) % NX * NCORE + c) for x in range(NX) for c in range(NCORE)]


def other_core():
    return [(x * NCORE + c, x * NCORE + 1 - c) for x in range(NX) for c in range(NCORE)]


def list_pairs(offsets, info, list_q, list_acc, list_k):
    rank = info[0]
    my_y, my_z = rank // NZ, rank % NZ

    def of_slot(slot):
        pos = info[1 + slot]
        return pos, info[1 + NGR + pos]

    query = []
    for i in range(NQ):
        slot = ((my_y + i // PER_RANK) % NY * NZ + my_z) * PER_RANK + i % PER_RANK
        pos, clip = of_slot(slot)
        query.append((pos, clip, info[1 + 2 * NGR + clip]))
    count = jnp.int32(0)
    for j, offset in enumerate(offsets):
        for g in range(PER_RANK):
            slot = (my_y * NZ + (my_z + offset) % NZ) * PER_RANK + g
            pos, clip = of_slot(slot)
            for i in range(NQ):
                q_pos, q_clip, q_kind = query[i]
                seen = (q_clip == clip) & ((q_kind == 1) | (pos <= q_pos))
                list_q[count] = i
                list_acc[count] = i
                list_k[count] = j * PER_RANK + g
                count = count + seen.astype(jnp.int32)
    for e in range(UNROLL + AHEAD):
        list_q[count + e] = 0
        list_acc[count + e] = TRASH
        list_k[count + e] = 0
    return count


def prepare(kv, query, keys, vals, turned):
    for g in range(PER_RANK):
        rows = pl.ds(g * GROUP, GROUP)
        turned[g] = query[rows, :].T
        keys[g] = kv[0, rows, :]
        vals[g] = kv[1, rows, :].T


def turn(*refs):
    *blocks, turned = refs
    for b, block in enumerate(blocks):
        for g in range(PER_RANK):
            turned[b * PER_RANK + g] = block[pl.ds(g * GROUP, GROUP), :].T


def attend(offsets, key_parts, first, last, *refs):
    refs = list(refs)

    def take(n):
        taken = refs[:n]
        del refs[:n]
        return taken

    (info,) = take(1)
    q_refs = take(2 if first else 1)
    block_refs = take(sum(key_parts))
    if not first:
        take(3)
    if last:
        out_refs = take(NY)
    acc, run_max, run_sum = take(3)
    (qt,) = take(1) if first else q_refs
    keys, vals, scores, list_q, list_acc, list_k = refs

    count = list_pairs(offsets, info, list_q, list_acc, list_k)

    if first:
        for i in range(NQ):
            qt[i] = q_refs[0][i] if i < PER_RANK else q_refs[1][i - PER_RANK]
    at = 0
    for j, parts in enumerate(key_parts):
        if parts == 1:
            key_block, value_block = block_refs[at].at[0], block_refs[at].at[1]
        else:
            key_block, value_block = block_refs[at], block_refs[at + 1]
        at += parts
        for g in range(PER_RANK):
            rows = pl.ds(g * GROUP, GROUP)
            if len(key_block.shape) == 3:
                keys[j * PER_RANK + g] = key_block[g]
                vals[j * PER_RANK + g] = value_block[g]
            else:
                keys[j * PER_RANK + g] = key_block[rows, :]
                vals[j * PER_RANK + g] = value_block[rows, :].T
    if first:
        acc[...] = jnp.zeros(acc.shape, F32)
        run_max[...] = jnp.full(run_max.shape, LOWEST, F32)
        run_sum[...] = jnp.zeros(run_sum.shape, F32)

    def score(t):
        return jnp.dot(keys[list_k[t]], qt[list_q[t]], preferred_element_type=F32)

    for t in range(AHEAD):
        scores[t] = score(t)

    def one_pair(t, slot):
        scores[(slot + AHEAD) % (AHEAD + 1)] = score(t + AHEAD)
        i = list_acc[t]
        tile = scores[slot % (AHEAD + 1)]
        old_max = run_max[i][:1]
        new_max = jnp.maximum(old_max, jnp.max(tile, axis=0, keepdims=True) * LOG2_SCALE)
        shrink = jnp.exp2(old_max - new_max)
        weights = jnp.exp2(tile * LOG2_SCALE - new_max)
        run_sum[i] = run_sum[i] * shrink + jnp.sum(weights.reshape(GROUP // 8, 8, GROUP), axis=0)
        acc[i] = acc[i] * shrink + jnp.dot(
            vals[list_k[t]], weights.astype(BF16), preferred_element_type=F32
        )
        run_max[i] = jnp.broadcast_to(new_max, (8, GROUP))

    def some_pairs(t, carry):
        for u in range(UNROLL):
            one_pair(UNROLL * t + u, u)
        return carry

    lax.fori_loop(0, (count + UNROLL - 1) // UNROLL, some_pairs, 0)

    if last:
        row = lax.broadcasted_iota(jnp.int32, (STAT_ROWS, GROUP), 0)
        for i in range(NQ):
            total = jnp.sum(run_sum[i], axis=0, keepdims=True)
            some = total > 0
            total = jnp.where(some, total, 1.0)
            level = jnp.where(some, run_max[i][:1] + jnp.log2(total), LOWEST)
            high = level.astype(BF16).astype(F32)
            middle = (level - high).astype(BF16).astype(F32)
            low = level - high - middle
            g = i % PER_RANK
            for piece, value in enumerate((high, middle, low)):
                stats = jnp.where(row == g * STAT_PIECES + piece, value, stats if g + piece else 0.0)
            out = out_refs[i // PER_RANK]
            out[pl.ds(g * HEAD_DIM, HEAD_DIM), :] = (acc[i] / total).astype(BF16)
            if g == PER_RANK - 1:
                out[pl.ds(PER_RANK * HEAD_DIM, STAT_ROWS), :] = stats.astype(BF16)


def attend_call(offsets, info, queries, blocks, state, last):
    first = state is None
    n_keys = len(offsets) * PER_RANK
    key_parts = tuple(len(b) for b in blocks)
    state_shapes = [(NQ + 1, HEAD_DIM, GROUP), (NQ + 1, 8, GROUP), (NQ + 1, 8, GROUP)]
    operands = [info] + list(queries) + [a for b in blocks for a in b] + list(state or ())
    out_shape = [jax.ShapeDtypeStruct(s, F32) for s in state_shapes]
    if last:
        out_shape = [jax.ShapeDtypeStruct((PER_RANK * HEAD_DIM + STAT_ROWS, GROUP), BF16)] * NY + out_shape
    if first:
        out_shape += [jax.ShapeDtypeStruct((NQ, HEAD_DIM, GROUP), BF16)]
    pairs = NQ * n_keys
    list_len = pairs + UNROLL + AHEAD
    scratch = [
        pltpu.VMEM((n_keys, GROUP, HEAD_DIM), BF16),
        pltpu.VMEM((n_keys, HEAD_DIM, GROUP), BF16),
        pltpu.VMEM((AHEAD + 1, GROUP, GROUP), F32),
    ] + [pltpu.SMEM((list_len,), jnp.int32)] * 3
    return pl.pallas_call(
        functools.partial(attend, offsets, key_parts, first, last),
        name="attend_" + "_".join(str(o % NZ) for o in offsets),
        in_specs=[SMEM] + [VMEM] * (len(operands) - 1),
        out_specs=[VMEM] * len(out_shape),
        out_shape=out_shape,
        scratch_shapes=scratch,
        compiler_params=PARAMS,
        input_output_aliases={} if first else {len(operands) - 3 + i: NY * last + i for i in range(3)},
        cost_estimate=pl.CostEstimate(
            flops=pairs * GROUP * GROUP * HEAD_DIM * 4,
            bytes_accessed=4 << 20,
            transcendentals=pairs * GROUP * GROUP // 2,
        ),
    )(*operands)


def merge(*refs):
    *parts, out = refs
    for g in range(PER_RANK):
        levels = []
        for part in parts:
            stats = part[PER_RANK * HEAD_DIM :, :].astype(F32)
            levels.append(sum(stats[g * STAT_PIECES + p : g * STAT_PIECES + p + 1] for p in range(STAT_PIECES)))
        top = functools.reduce(jnp.maximum, levels)
        shares = [jnp.exp2(level - top) for level in levels]
        whole = functools.reduce(jnp.add, shares)
        total = functools.reduce(
            jnp.add,
            [part[g * HEAD_DIM : (g + 1) * HEAD_DIM, :].astype(F32) * (share / whole) for part, share in zip(parts, shares)],
        )
        out[pl.ds(g * GROUP, GROUP), :] = total.T.astype(BF16)


def project(steps, final, head_ref, *refs):
    refs = list(refs)
    out, rows = refs[-2:]
    weight = refs[-3]
    blocks = refs[: NCORE * len(steps)]
    me = head_ref[0]
    my_x, my_core = me // NCORE, me % NCORE
    width = NCORE * HEAD_DIM
    for n, step in enumerate(steps):
        for side in range(NCORE):
            core = (my_core + side) % NCORE
            column = pl.multiple_of(n * width + core * HEAD_DIM, HEAD_DIM)
            rows[:, pl.ds(column, HEAD_DIM)] = blocks[n * NCORE + side][...]
    total = refs[len(blocks)][...] if final else 0.0
    for n, step in enumerate(steps):
        chip = (my_x + NX - step) % NX
        total = total + jnp.dot(
            rows[:, n * width : (n + 1) * width],
            weight[pl.ds(pl.multiple_of(chip * width, width), width), :],
            preferred_element_type=F32,
        )
    out[...] = total.astype(out.dtype)


def project_call(steps, head, blocks, sofar, out_weight):
    final = sofar is not None
    tok_dev, out_width = blocks[0].shape[0], out_weight.shape[1]
    operands = list(blocks) + ([sofar] if final else []) + [out_weight]
    return pl.pallas_call(
        functools.partial(project, steps, final),
        name="project_" + "_".join(map(str, steps)),
        in_specs=[SMEM] + [VMEM] * len(operands),
        out_specs=VMEM,
        out_shape=jax.ShapeDtypeStruct((tok_dev, out_width), BF16 if final else F32),
        scratch_shapes=[pltpu.VMEM((tok_dev, len(blocks) * HEAD_DIM), BF16)],
        compiler_params=PARAMS,
        cost_estimate=pl.CostEstimate(
            flops=2 * tok_dev * out_width * HEAD_DIM * len(blocks),
            bytes_accessed=4 << 20,
            transcendentals=0,
        ),
    )(head, *operands)


def shards(queries, keys_values, out_weight, group_owner, clip_ids, mask_types):
    tok_dev = queries.shape[0]
    rank = lax.axis_index("ctx").astype(jnp.int32).reshape(1)
    head = lax.axis_index("head").astype(jnp.int32).reshape(1)

    def onward(right, left):
        return lax.ppermute(right, "ctx", along_z(1)), lax.ppermute(left, "ctx", along_z(-1))

    right, left = onward(keys_values, keys_values)
    all_q = [lax.ppermute(queries, "ctx", along_y(-d)) for d in range(1, NY)]
    info = jnp.concatenate([rank, group_owner, clip_ids, mask_types])
    *own, own_q = pl.pallas_call(
        prepare,
        name="prepare",
        in_specs=[VMEM] * 2,
        out_specs=[VMEM] * 3,
        out_shape=[
            jax.ShapeDtypeStruct((PER_RANK, GROUP, HEAD_DIM), BF16),
            jax.ShapeDtypeStruct((PER_RANK, HEAD_DIM, GROUP), BF16),
            jax.ShapeDtypeStruct((PER_RANK, HEAD_DIM, GROUP), BF16),
        ],
        compiler_params=pltpu.CompilerParams(vmem_limit_bytes=8 << 20),
    )(keys_values, queries)
    others_q = pl.pallas_call(
        turn,
        name="turn",
        in_specs=[VMEM] * len(all_q),
        out_specs=VMEM,
        out_shape=jax.ShapeDtypeStruct((NQ - PER_RANK, HEAD_DIM, GROUP), BF16),
        compiler_params=pltpu.CompilerParams(vmem_limit_bytes=8 << 20),
        cost_estimate=pl.CostEstimate(flops=1 << 20, bytes_accessed=1 << 20, transcendentals=0),
    )(*all_q)
    all_q = [own_q, others_q]
    right, left, info, own = lax.optimization_barrier((right, left, info, own))

    next_right, next_left = onward(right, left)
    *state, q_turned = attend_call((0, -1, 1), info, all_q, [own, (right,), (left,)], None, False)
    right, left, state = lax.optimization_barrier((next_right, next_left, state))

    next_right, next_left = onward(right, left)
    state = attend_call((-2, 2), info, [q_turned], [(right,), (left,)], state, False)
    right, left, state = lax.optimization_barrier((next_right, next_left, state))

    far = onward(right[0], left[1])
    state = attend_call((-3, 3), info, [q_turned], [(right,), (left,)], state, False)
    parts = attend_call((4,), info, [q_turned], [far], state, True)[:NY]

    parts = [parts[0]] + [lax.ppermute(parts[d], "ctx", along_y(d)) for d in range(1, NY)]
    attended = pl.pallas_call(
        merge,
        name="merge",
        in_specs=[VMEM] * NY,
        out_specs=VMEM,
        out_shape=jax.ShapeDtypeStruct((tok_dev, HEAD_DIM), BF16),
        compiler_params=PARAMS,
    )(*parts)

    blocks = []
    for d in range(NX):
        block = attended if d == 0 else lax.ppermute(attended, "head", along_x(d))
        blocks.append([block, lax.ppermute(block, "head", other_core())])
    sofar = project_call((0, 1, 3), head, blocks[0] + blocks[1] + blocks[3], None, out_weight)
    return project_call((2,), head, blocks[2], sofar, out_weight)


def solution(mesh):
    placed = (P("ctx", "head"), P(None, "ctx", "head"), P(None, "head"), P(), P(), P())
    return jax.shard_map(
        shards, mesh=mesh, in_specs=placed, out_specs=P("ctx", "head"), check_vma=False
    )
```

```python
import functools
import math

import jax
import jax.numpy as jnp
from jax import lax
from jax.experimental import pallas as pl
from jax.experimental.pallas import tpu as pltpu
from jax.sharding import PartitionSpec as P

HEAD_DIM = 128
GROUP = 384
PER_RANK = 2
NY, NZ = 4, 8
NX, NCORE = 4, 2
NGR = NY * NZ * PER_RANK
NQ = NY * PER_RANK
EVERY = tuple(range(NY))
TRASH = NQ
STAT_ROWS = 16
STAT_PIECES = 3
LOG2_SCALE = math.log2(math.e) / math.sqrt(HEAD_DIM)
LOWEST = -1e30
UNROLL = 3
AHEAD = 2
OUT_CHUNKS = 4
EARLY_STEPS, LATE_STEP = (0, 3, 2), 1
F32, BF16 = jnp.float32, jnp.bfloat16

SMEM = pl.BlockSpec(memory_space=pltpu.SMEM)
VMEM = pl.BlockSpec(memory_space=pltpu.VMEM)
PARAMS = pltpu.CompilerParams(vmem_limit_bytes=40 << 20)


def along_y(step):
    return [(y * NZ + z, (y + step) % NY * NZ + z) for y in range(NY) for z in range(NZ)]


def along_z(step):
    return [(y * NZ + z, y * NZ + (z + step) % NZ) for y in range(NY) for z in range(NZ)]


def along_x(step):
    return [(x * NCORE + c, (x + step) % NX * NCORE + c) for x in range(NX) for c in range(NCORE)]


def other_core():
    return [(x * NCORE + c, x * NCORE + 1 - c) for x in range(NX) for c in range(NCORE)]


def list_pairs(offsets, q_blocks, info, list_q, list_acc, list_k):
    rank = info[0]
    my_y, my_z = rank // NZ, rank % NZ

    def of_slot(slot):
        pos = info[1 + slot]
        return pos, info[1 + NGR + pos]

    query = []
    for b in q_blocks:
        for g in range(PER_RANK):
            pos, clip = of_slot(((my_y + b) % NY * NZ + my_z) * PER_RANK + g)
            query.append((b * PER_RANK + g, pos, clip, info[1 + 2 * NGR + clip]))
    count = jnp.int32(0)
    for j, offset in enumerate(offsets):
        for g in range(PER_RANK):
            slot = (my_y * NZ + (my_z + offset) % NZ) * PER_RANK + g
            pos, clip = of_slot(slot)
            for i, q_pos, q_clip, q_kind in query:
                seen = (q_clip == clip) & ((q_kind == 1) | (pos <= q_pos))
                list_q[count] = i
                list_acc[count] = i
                list_k[count] = j * PER_RANK + g
                count = count + seen.astype(jnp.int32)
    for e in range(UNROLL + AHEAD):
        list_q[count + e] = 0
        list_acc[count + e] = TRASH
        list_k[count + e] = 0
    return count


def prepare(kv, query, keys, vals, turned):
    for g in range(PER_RANK):
        rows = pl.ds(g * GROUP, GROUP)
        turned[g] = query[rows, :].T
        keys[g] = kv[0, rows, :]
        vals[g] = kv[1, rows, :].T


def turn(*refs):
    *blocks, turned = refs
    for b, block in enumerate(blocks):
        for g in range(PER_RANK):
            turned[b * PER_RANK + g] = block[pl.ds(g * GROUP, GROUP), :].T


def attend(offsets, q_blocks, key_parts, first, last, *refs):
    refs = list(refs)

    def take(n):
        taken = refs[:n]
        del refs[:n]
        return taken

    (info_in,) = take(1)
    q_refs = take(2 if first else 1)
    block_refs = take(sum(key_parts))
    if not first:
        take(3)
    if last:
        out_refs = dict(zip(q_blocks, take(len(q_blocks))))
    acc, run_max, run_sum = take(3)
    (qt,) = take(1) if first else q_refs
    keys, vals, scores, list_q, list_acc, list_k, info, info_sem = refs

    info_copy = pltpu.make_async_copy(info_in, info, info_sem)
    info_copy.start()
    if first:
        for i in range(NQ):
            qt[i] = q_refs[0][i] if i < PER_RANK else q_refs[1][i - PER_RANK]
    at = 0
    for j, parts in enumerate(key_parts):
        if parts == 1:
            key_block, value_block = block_refs[at].at[0], block_refs[at].at[1]
        else:
            key_block, value_block = block_refs[at], block_refs[at + 1]
        at += parts
        for g in range(PER_RANK):
            rows = pl.ds(g * GROUP, GROUP)
            if len(key_block.shape) == 3:
                keys[j * PER_RANK + g] = key_block[g]
                vals[j * PER_RANK + g] = value_block[g]
            else:
                keys[j * PER_RANK + g] = key_block[rows, :]
                vals[j * PER_RANK + g] = value_block[rows, :].T
    if first:
        acc[...] = jnp.zeros(acc.shape, F32)
        run_max[...] = jnp.full(run_max.shape, LOWEST, F32)
        run_sum[...] = jnp.zeros(run_sum.shape, F32)

    info_copy.wait()
    count = list_pairs(offsets, q_blocks, info, list_q, list_acc, list_k)

    def score(t):
        return jnp.dot(keys[list_k[t]], qt[list_q[t]], preferred_element_type=F32)

    for t in range(AHEAD):
        scores[t] = score(t)

    def one_pair(t, slot):
        scores[(slot + AHEAD) % (AHEAD + 1)] = score(t + AHEAD)
        i = list_acc[t]
        tile = scores[slot % (AHEAD + 1)]
        old_max = run_max[i][:1]
        new_max = jnp.maximum(old_max, jnp.max(tile, axis=0, keepdims=True) * LOG2_SCALE)
        shrink = jnp.exp2(old_max - new_max)
        weights = jnp.exp2(tile * LOG2_SCALE - new_max)
        run_sum[i] = run_sum[i] * shrink + jnp.sum(weights.reshape(GROUP // 8, 8, GROUP), axis=0)
        acc[i] = acc[i] * shrink + jnp.dot(
            vals[list_k[t]], weights.astype(BF16), preferred_element_type=F32
        )
        run_max[i] = jnp.broadcast_to(new_max, (8, GROUP))

    def some_pairs(t, carry):
        for u in range(UNROLL):
            one_pair(UNROLL * t + u, u)
        return carry

    lax.fori_loop(0, (count + UNROLL - 1) // UNROLL, some_pairs, 0)

    if last:
        row = lax.broadcasted_iota(jnp.int32, (STAT_ROWS, GROUP), 0)
        for i in [b * PER_RANK + g for b in q_blocks for g in range(PER_RANK)]:
            total = jnp.sum(run_sum[i], axis=0, keepdims=True)
            some = total > 0
            total = jnp.where(some, total, 1.0)
            level = jnp.where(some, run_max[i][:1] + jnp.log2(total), LOWEST)
            high = level.astype(BF16).astype(F32)
            middle = (level - high).astype(BF16).astype(F32)
            low = level - high - middle
            g = i % PER_RANK
            for piece, value in enumerate((high, middle, low)):
                stats = jnp.where(row == g * STAT_PIECES + piece, value, stats if g + piece else 0.0)
            out = out_refs[i // PER_RANK]
            out[pl.ds(g * HEAD_DIM, HEAD_DIM), :] = (acc[i] * (1.0 / total)).astype(BF16)
            if g == PER_RANK - 1:
                out[pl.ds(PER_RANK * HEAD_DIM, STAT_ROWS), :] = stats.astype(BF16)


def attend_call(offsets, q_blocks, info, queries, blocks, state, last):
    first = state is None
    n_keys = len(offsets) * PER_RANK
    key_parts = tuple(len(b) for b in blocks)
    state_shapes = [(NQ + 1, HEAD_DIM, GROUP), (NQ + 1, 8, GROUP), (NQ + 1, 8, GROUP)]
    operands = [info] + list(queries) + [a for b in blocks for a in b] + list(state or ())
    out_shape = [jax.ShapeDtypeStruct(s, F32) for s in state_shapes]
    if last:
        out_shape = [jax.ShapeDtypeStruct((PER_RANK * HEAD_DIM + STAT_ROWS, GROUP), BF16)] * len(q_blocks) + out_shape
    if first:
        out_shape += [jax.ShapeDtypeStruct((NQ, HEAD_DIM, GROUP), BF16)]
    pairs = len(q_blocks) * PER_RANK * n_keys
    list_len = pairs + UNROLL + AHEAD
    scratch = [
        pltpu.VMEM((n_keys, GROUP, HEAD_DIM), BF16),
        pltpu.VMEM((n_keys, HEAD_DIM, GROUP), BF16),
        pltpu.VMEM((AHEAD + 1, GROUP, GROUP), F32),
    ] + [pltpu.SMEM((list_len,), jnp.int32)] * 3
    scratch += [pltpu.SMEM(info.shape, jnp.int32), pltpu.SemaphoreType.DMA]
    return pl.pallas_call(
        functools.partial(attend, offsets, q_blocks, key_parts, first, last),
        name="attend_" + "_".join(str(o % NZ) for o in offsets) + "_q" + str(len(q_blocks)),
        in_specs=[pl.BlockSpec(memory_space=pl.ANY)] + [VMEM] * (len(operands) - 1),
        out_specs=[VMEM] * len(out_shape),
        out_shape=out_shape,
        scratch_shapes=scratch,
        compiler_params=PARAMS,
        input_output_aliases={} if first else {len(operands) - 3 + i: len(q_blocks) * last + i for i in range(3)},
        cost_estimate=pl.CostEstimate(
            flops=pairs * GROUP * GROUP * HEAD_DIM * 4,
            bytes_accessed=4 << 20,
            transcendentals=pairs * GROUP * GROUP // 2,
        ),
    )(*operands)


def merge(*refs):
    *parts, out = refs
    for g in range(PER_RANK):
        levels = []
        for part in parts:
            stats = part[PER_RANK * HEAD_DIM :, :].astype(F32)
            levels.append(sum(stats[g * STAT_PIECES + p : g * STAT_PIECES + p + 1] for p in range(STAT_PIECES)))
        top = functools.reduce(jnp.maximum, levels)
        shares = [jnp.exp2(level - top) for level in levels]
        whole = functools.reduce(jnp.add, shares)
        total = functools.reduce(
            jnp.add,
            [part[g * HEAD_DIM : (g + 1) * HEAD_DIM, :].astype(F32) * (share / whole) for part, share in zip(parts, shares)],
        )
        out[pl.ds(g * GROUP, GROUP), :] = total.T.astype(BF16)


def project_most(head_ref, *refs):
    *blocks, weight, sofar, late_weight, rows = refs
    me = head_ref[0]
    my_x, my_core = me // NCORE, me % NCORE
    width = NCORE * HEAD_DIM

    def weight_rows(step, side):
        head = (my_x + NX - step) % NX * NCORE + (my_core + side) % NCORE
        return pl.ds(pl.multiple_of(head * HEAD_DIM, HEAD_DIM), HEAD_DIM)

    total = 0.0
    for n, step in enumerate(EARLY_STEPS):
        for side in range(NCORE):
            column = pl.multiple_of(n * width + (my_core + side) % NCORE * HEAD_DIM, HEAD_DIM)
            rows[:, pl.ds(column, HEAD_DIM)] = blocks[n * NCORE + side][...]
        chip = (my_x + NX - step) % NX
        total = total + jnp.dot(
            rows[:, n * width : (n + 1) * width],
            weight[pl.ds(pl.multiple_of(chip * width, width), width), :],
            preferred_element_type=F32,
        )
    sofar[...] = total
    for side in range(NCORE):
        late_weight[side * HEAD_DIM : (side + 1) * HEAD_DIM, :] = weight[weight_rows(LATE_STEP, side), :]


def project_rest(block, passed, sofar, weight, out, rows, staged, sems):
    rows[:, :HEAD_DIM] = block[...]
    rows[:, HEAD_DIM:] = passed[...]
    height = rows.shape[0] // OUT_CHUNKS
    copies = []
    for k in range(OUT_CHUNKS):
        some = pl.ds(k * height, height)
        total = sofar[some, :] + jnp.dot(rows[some, :], weight[...], preferred_element_type=F32)
        staged[some, :] = total.astype(BF16)
        copies.append(pltpu.make_async_copy(staged.at[some, :], out.at[some, :], sems.at[k]))
        copies[-1].start()
    for copy in copies:
        copy.wait()


def project_call(head, pairs, out_weight):
    early = [block for step in EARLY_STEPS for block in pairs[step]]
    tok_dev, out_width = early[0].shape[0], out_weight.shape[1]
    width = NCORE * HEAD_DIM
    sofar, late_weight = pl.pallas_call(
        project_most,
        name="project_most",
        in_specs=[SMEM] + [VMEM] * (len(early) + 1),
        out_specs=[VMEM] * 2,
        out_shape=[
            jax.ShapeDtypeStruct((tok_dev, out_width), F32),
            jax.ShapeDtypeStruct((width, out_width), BF16),
        ],
        scratch_shapes=[pltpu.VMEM((tok_dev, len(early) * HEAD_DIM), BF16)],
        compiler_params=PARAMS,
        cost_estimate=pl.CostEstimate(
            flops=2 * tok_dev * out_width * HEAD_DIM * len(early), bytes_accessed=4 << 20, transcendentals=0
        ),
    )(head, *early, out_weight)
    return pl.pallas_call(
        project_rest,
        name="project_rest",
        in_specs=[VMEM] * 4,
        out_specs=pl.BlockSpec(memory_space=pl.ANY),
        out_shape=jax.ShapeDtypeStruct((tok_dev, out_width), BF16),
        scratch_shapes=[
            pltpu.VMEM((tok_dev, width), BF16),
            pltpu.VMEM((tok_dev, out_width), BF16),
            pltpu.SemaphoreType.DMA((OUT_CHUNKS,)),
        ],
        compiler_params=PARAMS,
    )(*pairs[LATE_STEP], sofar, late_weight)


def shards(queries, keys_values, out_weight, group_owner, clip_ids, mask_types):
    tok_dev = queries.shape[0]
    rank = lax.axis_index("ctx").astype(jnp.int32).reshape(1)
    head = lax.axis_index("head").astype(jnp.int32).reshape(1)

    def onward(right, left):
        return lax.ppermute(right, "ctx", along_z(1)), lax.ppermute(left, "ctx", along_z(-1))

    right, left = onward(keys_values, keys_values)
    all_q = [lax.ppermute(queries, "ctx", along_y(-d)) for d in range(1, NY)]
    info = jnp.concatenate([rank, group_owner, clip_ids, mask_types])
    *own, own_q = pl.pallas_call(
        prepare,
        name="prepare",
        in_specs=[VMEM] * 2,
        out_specs=[VMEM] * 3,
        out_shape=[
            jax.ShapeDtypeStruct((PER_RANK, GROUP, HEAD_DIM), BF16),
            jax.ShapeDtypeStruct((PER_RANK, HEAD_DIM, GROUP), BF16),
            jax.ShapeDtypeStruct((PER_RANK, HEAD_DIM, GROUP), BF16),
        ],
        compiler_params=pltpu.CompilerParams(vmem_limit_bytes=8 << 20),
    )(keys_values, queries)
    others_q = pl.pallas_call(
        turn,
        name="turn",
        in_specs=[VMEM] * len(all_q),
        out_specs=VMEM,
        out_shape=jax.ShapeDtypeStruct((NQ - PER_RANK, HEAD_DIM, GROUP), BF16),
        compiler_params=pltpu.CompilerParams(vmem_limit_bytes=8 << 20),
        cost_estimate=pl.CostEstimate(flops=1 << 20, bytes_accessed=1 << 20, transcendentals=0),
    )(*all_q)
    all_q = [own_q, others_q]
    right, left, info, own = lax.optimization_barrier((right, left, info, own))

    next_right, next_left = onward(right, left)
    *state, q_turned = attend_call((0, -1, 1), EVERY, info, all_q, [own, (right,), (left,)], None, False)
    right, left, state = lax.optimization_barrier((next_right, next_left, state))

    next_right, next_left = onward(right, left)
    state = attend_call((-2, 2), EVERY, info, [q_turned], [(right,), (left,)], state, False)
    right, left, state = lax.optimization_barrier((next_right, next_left, state))

    far = onward(right[0], left[1])
    state = attend_call((-3, 3), EVERY, info, [q_turned], [(right,), (left,)], state, False)
    away = (2, 1, 3)
    *sent, acc, run_max, run_sum = attend_call((4,), away, info, [q_turned], [far], state, True)
    parts = [lax.ppermute(part, "ctx", along_y(d)) for d, part in zip(away, sent)]
    parts.append(attend_call((4,), (0,), info, [q_turned], [far], (acc, run_max, run_sum), True)[0])
    attended = pl.pallas_call(
        merge,
        name="merge",
        in_specs=[VMEM] * NY,
        out_specs=VMEM,
        out_shape=jax.ShapeDtypeStruct((tok_dev, HEAD_DIM), BF16),
        compiler_params=PARAMS,
    )(*parts)

    blocks = []
    for d in range(NX):
        block = attended if d == 0 else lax.ppermute(attended, "head", along_x(d))
        blocks.append([block, lax.ppermute(block, "head", other_core())])
    return project_call(head, blocks, out_weight)


def solution(mesh):
    placed = (P("ctx", "head"), P(None, "ctx", "head"), P(None, "head"), P(), P(), P())
    return jax.shard_map(
        shards, mesh=mesh, in_specs=placed, out_specs=P("ctx", "head"), check_vma=False
    )
```

```python
import functools
import math

import jax
import jax.numpy as jnp
from jax import lax
from jax.experimental import pallas as pl
from jax.experimental.pallas import tpu as pltpu
from jax.sharding import PartitionSpec as P

HEAD_DIM = 128
GROUP = 384
PER_RANK = 2
NY, NZ = 4, 8
NX, NCORE = 4, 2
NGR = NY * NZ * PER_RANK
NQ = NY * PER_RANK
EVERY = tuple(range(NY))
TRASH = NQ
STAT_ROWS = 16
STAT_PIECES = 3
LOG2_SCALE = math.log2(math.e) / math.sqrt(HEAD_DIM)
LOWEST = -1e30
UNROLL = 3
AHEAD = 2
OUT_CHUNKS = 4
EARLY_STEPS, LATE_STEP = (0, 3, 2), 1
F32, BF16 = jnp.float32, jnp.bfloat16

SMEM = pl.BlockSpec(memory_space=pltpu.SMEM)
VMEM = pl.BlockSpec(memory_space=pltpu.VMEM)
PARAMS = pltpu.CompilerParams(vmem_limit_bytes=40 << 20)


def along_y(step):
    return [(y * NZ + z, (y + step) % NY * NZ + z) for y in range(NY) for z in range(NZ)]


def along_z(step):
    return [(y * NZ + z, y * NZ + (z + step) % NZ) for y in range(NY) for z in range(NZ)]


def along_x(step):
    return [(x * NCORE + c, (x + step) % NX * NCORE + c) for x in range(NX) for c in range(NCORE)]


def other_core():
    return [(x * NCORE + c, x * NCORE + 1 - c) for x in range(NX) for c in range(NCORE)]


def list_pairs(offsets, q_blocks, unroll, info, list_q, list_acc, list_k):
    rank = info[0]
    my_y, my_z = rank // NZ, rank % NZ

    def of_slot(slot):
        pos = info[1 + slot]
        return pos, info[1 + NGR + pos]

    query = []
    for b in q_blocks:
        for g in range(PER_RANK):
            pos, clip = of_slot(((my_y + b) % NY * NZ + my_z) * PER_RANK + g)
            query.append((b * PER_RANK + g, pos, clip, info[1 + 2 * NGR + clip]))
    count = jnp.int32(0)
    for j, offset in enumerate(offsets):
        for g in range(PER_RANK):
            slot = (my_y * NZ + (my_z + offset) % NZ) * PER_RANK + g
            pos, clip = of_slot(slot)
            for i, q_pos, q_clip, q_kind in query:
                seen = (q_clip == clip) & ((q_kind == 1) | (pos <= q_pos))
                list_q[count] = i
                list_acc[count] = i
                list_k[count] = j * PER_RANK + g
                count = count + seen.astype(jnp.int32)
    for e in range(unroll + AHEAD):
        list_q[count + e] = 0
        list_acc[count + e] = TRASH
        list_k[count + e] = 0
    return count


def prepare(kv, query, keys, vals, turned):
    for g in range(PER_RANK):
        rows = pl.ds(g * GROUP, GROUP)
        turned[g] = query[rows, :].T
        keys[g] = kv[0, rows, :]
        vals[g] = kv[1, rows, :].T


def turn(*refs):
    *blocks, turned = refs
    for b, block in enumerate(blocks):
        for g in range(PER_RANK):
            turned[b * PER_RANK + g] = block[pl.ds(g * GROUP, GROUP), :].T


def attend(offsets, q_blocks, unroll, key_parts, first, last, *refs):
    refs = list(refs)

    def take(n):
        taken = refs[:n]
        del refs[:n]
        return taken

    (info_in,) = take(1)
    q_refs = take(2 if first else 1)
    block_refs = take(sum(key_parts))
    if not first:
        take(3)
    if last:
        out_refs = dict(zip(q_blocks, take(len(q_blocks))))
    acc, run_max, run_sum = take(3)
    (qt,) = take(1) if first else q_refs
    keys, vals, scores, list_q, list_acc, list_k, info, info_sem = refs

    info_copy = pltpu.make_async_copy(info_in, info, info_sem)
    info_copy.start()
    if first:
        for i in range(NQ):
            qt[i] = q_refs[0][i] if i < PER_RANK else q_refs[1][i - PER_RANK]
    at = 0
    for j, parts in enumerate(key_parts):
        if parts == 1:
            key_block, value_block = block_refs[at].at[0], block_refs[at].at[1]
        else:
            key_block, value_block = block_refs[at], block_refs[at + 1]
        at += parts
        for g in range(PER_RANK):
            rows = pl.ds(g * GROUP, GROUP)
            if len(key_block.shape) == 3:
                keys[j * PER_RANK + g] = key_block[g]
                vals[j * PER_RANK + g] = value_block[g]
            else:
                keys[j * PER_RANK + g] = key_block[rows, :]
                vals[j * PER_RANK + g] = value_block[rows, :].T
    if first:
        acc[...] = jnp.zeros(acc.shape, F32)
        run_max[...] = jnp.full(run_max.shape, LOWEST, F32)
        run_sum[...] = jnp.zeros(run_sum.shape, F32)

    info_copy.wait()
    count = list_pairs(offsets, q_blocks, unroll, info, list_q, list_acc, list_k)

    def score(t):
        return jnp.dot(keys[list_k[t]], qt[list_q[t]], preferred_element_type=F32)

    for t in range(AHEAD):
        scores[t] = score(t)

    def one_pair(t, slot):
        scores[(slot + AHEAD) % (AHEAD + 1)] = score(t + AHEAD)
        i = list_acc[t]
        tile = scores[slot % (AHEAD + 1)]
        old_max = run_max[i][:1]
        new_max = jnp.maximum(old_max, jnp.max(tile, axis=0, keepdims=True) * LOG2_SCALE)
        shrink = jnp.exp2(old_max - new_max)
        weights = jnp.exp2(tile * LOG2_SCALE - new_max)
        run_sum[i] = run_sum[i] * shrink + jnp.sum(weights.reshape(GROUP // 8, 8, GROUP), axis=0)
        acc[i] = acc[i] * shrink + jnp.dot(
            vals[list_k[t]], weights.astype(BF16), preferred_element_type=F32
        )
        run_max[i] = jnp.broadcast_to(new_max, (8, GROUP))

    def some_pairs(t, carry):
        for u in range(unroll):
            one_pair(unroll * t + u, u)
        return carry

    lax.fori_loop(0, (count + unroll - 1) // unroll, some_pairs, 0)

    if last:
        row = lax.broadcasted_iota(jnp.int32, (STAT_ROWS, GROUP), 0)
        for i in [b * PER_RANK + g for b in q_blocks for g in range(PER_RANK)]:
            total = jnp.sum(run_sum[i], axis=0, keepdims=True)
            some = total > 0
            total = jnp.where(some, total, 1.0)
            level = jnp.where(some, run_max[i][:1] + jnp.log2(total), LOWEST)
            high = level.astype(BF16).astype(F32)
            middle = (level - high).astype(BF16).astype(F32)
            low = level - high - middle
            g = i % PER_RANK
            for piece, value in enumerate((high, middle, low)):
                stats = jnp.where(row == g * STAT_PIECES + piece, value, stats if g + piece else 0.0)
            out = out_refs[i // PER_RANK]
            out[pl.ds(g * HEAD_DIM, HEAD_DIM), :] = (acc[i] * (1.0 / total)).astype(BF16)
            if g == PER_RANK - 1:
                out[pl.ds(PER_RANK * HEAD_DIM, STAT_ROWS), :] = stats.astype(BF16)


def attend_call(offsets, q_blocks, info, queries, blocks, state, last):
    first = state is None
    n_keys = len(offsets) * PER_RANK
    key_parts = tuple(len(b) for b in blocks)
    state_shapes = [(NQ + 1, HEAD_DIM, GROUP), (NQ + 1, 8, GROUP), (NQ + 1, 8, GROUP)]
    operands = [info] + list(queries) + [a for b in blocks for a in b] + list(state or ())
    out_shape = [jax.ShapeDtypeStruct(s, F32) for s in state_shapes]
    if last:
        out_shape = [jax.ShapeDtypeStruct((PER_RANK * HEAD_DIM + STAT_ROWS, GROUP), BF16)] * len(q_blocks) + out_shape
    if first:
        out_shape += [jax.ShapeDtypeStruct((NQ, HEAD_DIM, GROUP), BF16)]
    pairs = len(q_blocks) * PER_RANK * n_keys
    unroll = UNROLL * (2 if first else 1)
    list_len = pairs + unroll + AHEAD
    scratch = [
        pltpu.VMEM((n_keys, GROUP, HEAD_DIM), BF16),
        pltpu.VMEM((n_keys, HEAD_DIM, GROUP), BF16),
        pltpu.VMEM((AHEAD + 1, GROUP, GROUP), F32),
    ] + [pltpu.SMEM((list_len,), jnp.int32)] * 3
    scratch += [pltpu.SMEM(info.shape, jnp.int32), pltpu.SemaphoreType.DMA]
    return pl.pallas_call(
        functools.partial(attend, offsets, q_blocks, unroll, key_parts, first, last),
        name="attend_" + "_".join(str(o % NZ) for o in offsets) + "_q" + str(len(q_blocks)),
        in_specs=[pl.BlockSpec(memory_space=pl.ANY)] + [VMEM] * (len(operands) - 1),
        out_specs=[VMEM] * len(out_shape),
        out_shape=out_shape,
        scratch_shapes=scratch,
        compiler_params=PARAMS,
        input_output_aliases={} if first else {len(operands) - 3 + i: len(q_blocks) * last + i for i in range(3)},
        cost_estimate=pl.CostEstimate(
            flops=pairs * GROUP * GROUP * HEAD_DIM * 4,
            bytes_accessed=4 << 20,
            transcendentals=pairs * GROUP * GROUP // 2,
        ),
    )(*operands)


def merge(*refs):
    *parts, out = refs
    for g in range(PER_RANK):
        levels = []
        for part in parts:
            stats = part[PER_RANK * HEAD_DIM :, :].astype(F32)
            levels.append(sum(stats[g * STAT_PIECES + p : g * STAT_PIECES + p + 1] for p in range(STAT_PIECES)))
        top = functools.reduce(jnp.maximum, levels)
        shares = [jnp.exp2(level - top) for level in levels]
        whole = functools.reduce(jnp.add, shares)
        total = functools.reduce(
            jnp.add,
            [part[g * HEAD_DIM : (g + 1) * HEAD_DIM, :].astype(F32) * (share / whole) for part, share in zip(parts, shares)],
        )
        out[pl.ds(g * GROUP, GROUP), :] = total.T.astype(BF16)


def project_most(head_ref, *refs):
    *blocks, weight, sofar, late_weight, rows = refs
    me = head_ref[0]
    my_x, my_core = me // NCORE, me % NCORE
    width = NCORE * HEAD_DIM

    def weight_rows(step, side):
        head = (my_x + NX - step) % NX * NCORE + (my_core + side) % NCORE
        return pl.ds(pl.multiple_of(head * HEAD_DIM, HEAD_DIM), HEAD_DIM)

    total = 0.0
    for n, step in enumerate(EARLY_STEPS):
        for side in range(NCORE):
            column = pl.multiple_of(n * width + (my_core + side) % NCORE * HEAD_DIM, HEAD_DIM)
            rows[:, pl.ds(column, HEAD_DIM)] = blocks[n * NCORE + side][...]
        chip = (my_x + NX - step) % NX
        total = total + jnp.dot(
            rows[:, n * width : (n + 1) * width],
            weight[pl.ds(pl.multiple_of(chip * width, width), width), :],
            preferred_element_type=F32,
        )
    sofar[...] = total
    for side in range(NCORE):
        late_weight[side * HEAD_DIM : (side + 1) * HEAD_DIM, :] = weight[weight_rows(LATE_STEP, side), :]


def project_rest(block, passed, sofar, weight, out, rows, staged, sems):
    rows[:, :HEAD_DIM] = block[...]
    rows[:, HEAD_DIM:] = passed[...]
    height = rows.shape[0] // OUT_CHUNKS
    copies = []
    for k in range(OUT_CHUNKS):
        some = pl.ds(k * height, height)
        total = sofar[some, :] + jnp.dot(rows[some, :], weight[...], preferred_element_type=F32)
        staged[some, :] = total.astype(BF16)
        copies.append(pltpu.make_async_copy(staged.at[some, :], out.at[some, :], sems.at[k]))
        copies[-1].start()
    for copy in copies:
        copy.wait()


def project_call(head, pairs, out_weight):
    early = [block for step in EARLY_STEPS for block in pairs[step]]
    tok_dev, out_width = early[0].shape[0], out_weight.shape[1]
    width = NCORE * HEAD_DIM
    sofar, late_weight = pl.pallas_call(
        project_most,
        name="project_most",
        in_specs=[SMEM] + [VMEM] * (len(early) + 1),
        out_specs=[VMEM] * 2,
        out_shape=[
            jax.ShapeDtypeStruct((tok_dev, out_width), F32),
            jax.ShapeDtypeStruct((width, out_width), BF16),
        ],
        scratch_shapes=[pltpu.VMEM((tok_dev, len(early) * HEAD_DIM), BF16)],
        compiler_params=PARAMS,
        cost_estimate=pl.CostEstimate(
            flops=2 * tok_dev * out_width * HEAD_DIM * len(early), bytes_accessed=4 << 20, transcendentals=0
        ),
    )(head, *early, out_weight)
    return pl.pallas_call(
        project_rest,
        name="project_rest",
        in_specs=[VMEM] * 4,
        out_specs=pl.BlockSpec(memory_space=pl.ANY),
        out_shape=jax.ShapeDtypeStruct((tok_dev, out_width), BF16),
        scratch_shapes=[
            pltpu.VMEM((tok_dev, width), BF16),
            pltpu.VMEM((tok_dev, out_width), BF16),
            pltpu.SemaphoreType.DMA((OUT_CHUNKS,)),
        ],
        compiler_params=PARAMS,
    )(*pairs[LATE_STEP], sofar, late_weight)


def shards(queries, keys_values, out_weight, group_owner, clip_ids, mask_types):
    tok_dev = queries.shape[0]
    rank = lax.axis_index("ctx").astype(jnp.int32).reshape(1)
    head = lax.axis_index("head").astype(jnp.int32).reshape(1)

    def onward(right, left):
        return lax.ppermute(right, "ctx", along_z(1)), lax.ppermute(left, "ctx", along_z(-1))

    right, left = onward(keys_values, keys_values)
    all_q = [lax.ppermute(queries, "ctx", along_y(-d)) for d in range(1, NY)]
    info = jnp.concatenate([rank, group_owner, clip_ids, mask_types])
    *own, own_q = pl.pallas_call(
        prepare,
        name="prepare",
        in_specs=[VMEM] * 2,
        out_specs=[VMEM] * 3,
        out_shape=[
            jax.ShapeDtypeStruct((PER_RANK, GROUP, HEAD_DIM), BF16),
            jax.ShapeDtypeStruct((PER_RANK, HEAD_DIM, GROUP), BF16),
            jax.ShapeDtypeStruct((PER_RANK, HEAD_DIM, GROUP), BF16),
        ],
        compiler_params=pltpu.CompilerParams(vmem_limit_bytes=8 << 20),
    )(keys_values, queries)
    others_q = pl.pallas_call(
        turn,
        name="turn",
        in_specs=[VMEM] * len(all_q),
        out_specs=VMEM,
        out_shape=jax.ShapeDtypeStruct((NQ - PER_RANK, HEAD_DIM, GROUP), BF16),
        compiler_params=pltpu.CompilerParams(vmem_limit_bytes=8 << 20),
        cost_estimate=pl.CostEstimate(flops=1 << 20, bytes_accessed=1 << 20, transcendentals=0),
    )(*all_q)
    all_q = [own_q, others_q]
    right, left, info, own = lax.optimization_barrier((right, left, info, own))

    next_right, next_left = onward(right, left)
    *state, q_turned = attend_call((0, -1, 1), EVERY, info, all_q, [own, (right,), (left,)], None, False)
    right, left, state = lax.optimization_barrier((next_right, next_left, state))

    next_right, next_left = onward(right, left)
    state = attend_call((-2, 2), EVERY, info, [q_turned], [(right,), (left,)], state, False)
    right, left, state = lax.optimization_barrier((next_right, next_left, state))

    far = onward(right[0], left[1])
    state = attend_call((-3, 3), EVERY, info, [q_turned], [(right,), (left,)], state, False)
    away = (2, 1, 3)
    *sent, acc, run_max, run_sum = attend_call((4,), away, info, [q_turned], [far], state, True)
    parts = [lax.ppermute(part, "ctx", along_y(d)) for d, part in zip(away, sent)]
    parts.append(attend_call((4,), (0,), info, [q_turned], [far], (acc, run_max, run_sum), True)[0])
    attended = pl.pallas_call(
        merge,
        name="merge",
        in_specs=[VMEM] * NY,
        out_specs=VMEM,
        out_shape=jax.ShapeDtypeStruct((tok_dev, HEAD_DIM), BF16),
        compiler_params=PARAMS,
    )(*parts)

    blocks = []
    for d in range(NX):
        block = attended if d == 0 else lax.ppermute(attended, "head", along_x(d))
        blocks.append([block, lax.ppermute(block, "head", other_core())])
    return project_call(head, blocks, out_weight)


def solution(mesh):
    placed = (P("ctx", "head"), P(None, "ctx", "head"), P(None, "head"), P(), P(), P())
    return jax.shard_map(
        shards, mesh=mesh, in_specs=placed, out_specs=P("ctx", "head"), check_vma=False
    )
```

```python
import functools
import math

import jax
import jax.numpy as jnp
from jax import lax
from jax.experimental import pallas as pl
from jax.experimental.pallas import tpu as pltpu
from jax.sharding import PartitionSpec as P

HEAD_DIM = 128
GROUP = 384
PER_RANK = 2
NY, NZ = 4, 8
NX, NCORE = 4, 2
NGR = NY * NZ * PER_RANK
NQ = NY * PER_RANK
EVERY = tuple(range(NY))
TRASH = NQ
STAT_ROWS = 16
STAT_PIECES = 3
LOG2_SCALE = math.log2(math.e) / math.sqrt(HEAD_DIM)
LOWEST = -1e30
UNROLL = 3
AHEAD = 2
OUT_CHUNKS = 4
EARLY_STEPS, LATE_STEP = (0, 3, 2), 1
F32, BF16 = jnp.float32, jnp.bfloat16

SMEM = pl.BlockSpec(memory_space=pltpu.SMEM)
VMEM = pl.BlockSpec(memory_space=pltpu.VMEM)
PARAMS = pltpu.CompilerParams(vmem_limit_bytes=40 << 20)


def along_y(step):
    return [(y * NZ + z, (y + step) % NY * NZ + z) for y in range(NY) for z in range(NZ)]


def along_z(step):
    return [(y * NZ + z, y * NZ + (z + step) % NZ) for y in range(NY) for z in range(NZ)]


def along_x(step):
    return [(x * NCORE + c, (x + step) % NX * NCORE + c) for x in range(NX) for c in range(NCORE)]


def other_core():
    return [(x * NCORE + c, x * NCORE + 1 - c) for x in range(NX) for c in range(NCORE)]


def list_pairs(offsets, q_blocks, unroll, info, list_q, list_acc, list_k):
    rank = info[0]
    my_y, my_z = rank // NZ, rank % NZ

    def of_slot(slot):
        pos = info[1 + slot]
        return pos, info[1 + NGR + pos]

    query = []
    for b in q_blocks:
        for g in range(PER_RANK):
            pos, clip = of_slot(((my_y + b) % NY * NZ + my_z) * PER_RANK + g)
            query.append((b * PER_RANK + g, pos, clip, info[1 + 2 * NGR + clip]))
    count = jnp.int32(0)
    for j, offset in enumerate(offsets):
        for g in range(PER_RANK):
            slot = (my_y * NZ + (my_z + offset) % NZ) * PER_RANK + g
            pos, clip = of_slot(slot)
            for i, q_pos, q_clip, q_kind in query:
                seen = (q_clip == clip) & ((q_kind == 1) | (pos <= q_pos))
                list_q[count] = i
                list_acc[count] = i
                list_k[count] = j * PER_RANK + g
                count = count + seen.astype(jnp.int32)
    for e in range(unroll + AHEAD):
        list_q[count + e] = 0
        list_acc[count + e] = TRASH
        list_k[count + e] = 0
    return count


def prepare(kv, query, keys, vals, turned):
    for g in range(PER_RANK):
        rows = pl.ds(g * GROUP, GROUP)
        turned[g] = query[rows, :].T
        keys[g] = kv[0, rows, :]
        vals[g] = kv[1, rows, :].T


def turn(*refs):
    *blocks, turned = refs
    for b, block in enumerate(blocks):
        for g in range(PER_RANK):
            turned[b * PER_RANK + g] = block[pl.ds(g * GROUP, GROUP), :].T


def attend(offsets, q_blocks, unroll, key_parts, first, last, *refs):
    refs = list(refs)

    def take(n):
        taken = refs[:n]
        del refs[:n]
        return taken

    (info_in,) = take(1)
    q_refs = take(2 if first else 1)
    block_refs = take(sum(key_parts))
    if not first:
        take(3)
    if last:
        out_refs = dict(zip(q_blocks, take(len(q_blocks))))
    acc, run_max, run_sum = take(3)
    (qt,) = take(1) if first else q_refs
    keys, vals, scores, list_q, list_acc, list_k, info, info_sem = refs

    info_copy = pltpu.make_async_copy(info_in, info, info_sem)
    info_copy.start()
    if first:
        for i in range(NQ):
            qt[i] = q_refs[0][i] if i < PER_RANK else q_refs[1][i - PER_RANK]
    at = 0
    for j, parts in enumerate(key_parts):
        if parts == 1:
            key_block, value_block = block_refs[at].at[0], block_refs[at].at[1]
        else:
            key_block, value_block = block_refs[at], block_refs[at + 1]
        at += parts
        for g in range(PER_RANK):
            rows = pl.ds(g * GROUP, GROUP)
            if len(key_block.shape) == 3:
                keys[j * PER_RANK + g] = key_block[g]
                vals[j * PER_RANK + g] = value_block[g]
            else:
                keys[j * PER_RANK + g] = key_block[rows, :]
                vals[j * PER_RANK + g] = value_block[rows, :].T
    if first:
        acc[...] = jnp.zeros(acc.shape, F32)
        run_max[...] = jnp.full(run_max.shape, LOWEST, F32)
        run_sum[...] = jnp.zeros(run_sum.shape, F32)

    info_copy.wait()
    count = list_pairs(offsets, q_blocks, unroll, info, list_q, list_acc, list_k)

    def score(t):
        return jnp.dot(keys[list_k[t]], qt[list_q[t]], preferred_element_type=F32)

    for t in range(AHEAD):
        scores[t] = score(t)

    def one_pair(t, slot):
        scores[(slot + AHEAD) % (AHEAD + 1)] = score(t + AHEAD)
        i = list_acc[t]
        tile = scores[slot % (AHEAD + 1)]
        old_max = run_max[i][:1]
        new_max = jnp.maximum(old_max, jnp.max(tile, axis=0, keepdims=True) * LOG2_SCALE)
        shrink = jnp.exp2(old_max - new_max)
        weights = jnp.exp2(tile * LOG2_SCALE - new_max)
        run_sum[i] = run_sum[i] * shrink + jnp.sum(weights.reshape(GROUP // 8, 8, GROUP), axis=0)
        acc[i] = acc[i] * shrink + jnp.dot(
            vals[list_k[t]], weights.astype(BF16), preferred_element_type=F32
        )
        run_max[i] = jnp.broadcast_to(new_max, (8, GROUP))

    def pairs_from(base, width):
        def some_pairs(t, carry):
            for u in range(width):
                one_pair(base + width * t + u, u)
            return carry

        return some_pairs

    long_turns = count // unroll if unroll > UNROLL else 0
    done = long_turns * unroll
    if unroll > UNROLL:
        lax.fori_loop(0, long_turns, pairs_from(0, unroll), 0)
    lax.fori_loop(0, (count - done + UNROLL - 1) // UNROLL, pairs_from(done, UNROLL), 0)

    if last:
        row = lax.broadcasted_iota(jnp.int32, (STAT_ROWS, GROUP), 0)
        for i in [b * PER_RANK + g for b in q_blocks for g in range(PER_RANK)]:
            total = jnp.sum(run_sum[i], axis=0, keepdims=True)
            some = total > 0
            total = jnp.where(some, total, 1.0)
            level = jnp.where(some, run_max[i][:1] + jnp.log2(total), LOWEST)
            high = level.astype(BF16).astype(F32)
            middle = (level - high).astype(BF16).astype(F32)
            low = level - high - middle
            g = i % PER_RANK
            for piece, value in enumerate((high, middle, low)):
                stats = jnp.where(row == g * STAT_PIECES + piece, value, stats if g + piece else 0.0)
            out = out_refs[i // PER_RANK]
            out[pl.ds(g * HEAD_DIM, HEAD_DIM), :] = (acc[i] * (1.0 / total)).astype(BF16)
            if g == PER_RANK - 1:
                out[pl.ds(PER_RANK * HEAD_DIM, STAT_ROWS), :] = stats.astype(BF16)


def attend_call(offsets, q_blocks, info, queries, blocks, state, last):
    first = state is None
    n_keys = len(offsets) * PER_RANK
    key_parts = tuple(len(b) for b in blocks)
    state_shapes = [(NQ + 1, HEAD_DIM, GROUP), (NQ + 1, 8, GROUP), (NQ + 1, 8, GROUP)]
    operands = [info] + list(queries) + [a for b in blocks for a in b] + list(state or ())
    out_shape = [jax.ShapeDtypeStruct(s, F32) for s in state_shapes]
    if last:
        out_shape = [jax.ShapeDtypeStruct((PER_RANK * HEAD_DIM + STAT_ROWS, GROUP), BF16)] * len(q_blocks) + out_shape
    if first:
        out_shape += [jax.ShapeDtypeStruct((NQ, HEAD_DIM, GROUP), BF16)]
    pairs = len(q_blocks) * PER_RANK * n_keys
    unroll = UNROLL * (1 if last else 2)
    list_len = pairs + unroll + AHEAD
    scratch = [
        pltpu.VMEM((n_keys, GROUP, HEAD_DIM), BF16),
        pltpu.VMEM((n_keys, HEAD_DIM, GROUP), BF16),
        pltpu.VMEM((AHEAD + 1, GROUP, GROUP), F32),
    ] + [pltpu.SMEM((list_len,), jnp.int32)] * 3
    scratch += [pltpu.SMEM(info.shape, jnp.int32), pltpu.SemaphoreType.DMA]
    return pl.pallas_call(
        functools.partial(attend, offsets, q_blocks, unroll, key_parts, first, last),
        name="attend_" + "_".join(str(o % NZ) for o in offsets) + "_q" + str(len(q_blocks)),
        in_specs=[pl.BlockSpec(memory_space=pl.ANY)] + [VMEM] * (len(operands) - 1),
        out_specs=[VMEM] * len(out_shape),
        out_shape=out_shape,
        scratch_shapes=scratch,
        compiler_params=PARAMS,
        input_output_aliases={} if first else {len(operands) - 3 + i: len(q_blocks) * last + i for i in range(3)},
        cost_estimate=pl.CostEstimate(
            flops=pairs * GROUP * GROUP * HEAD_DIM * 4,
            bytes_accessed=4 << 20,
            transcendentals=pairs * GROUP * GROUP // 2,
        ),
    )(*operands)


def merge(*refs):
    *parts, out = refs
    for g in range(PER_RANK):
        levels = []
        for part in parts:
            stats = part[PER_RANK * HEAD_DIM :, :].astype(F32)
            levels.append(sum(stats[g * STAT_PIECES + p : g * STAT_PIECES + p + 1] for p in range(STAT_PIECES)))
        top = functools.reduce(jnp.maximum, levels)
        shares = [jnp.exp2(level - top) for level in levels]
        whole = functools.reduce(jnp.add, shares)
        total = functools.reduce(
            jnp.add,
            [part[g * HEAD_DIM : (g + 1) * HEAD_DIM, :].astype(F32) * (share / whole) for part, share in zip(parts, shares)],
        )
        out[pl.ds(g * GROUP, GROUP), :] = total.T.astype(BF16)


def project_most(head_ref, *refs):
    *blocks, weight, sofar, late_weight, rows = refs
    me = head_ref[0]
    my_x, my_core = me // NCORE, me % NCORE
    width = NCORE * HEAD_DIM

    def weight_rows(step, side):
        head = (my_x + NX - step) % NX * NCORE + (my_core + side) % NCORE
        return pl.ds(pl.multiple_of(head * HEAD_DIM, HEAD_DIM), HEAD_DIM)

    total = 0.0
    for n, step in enumerate(EARLY_STEPS):
        for side in range(NCORE):
            column = pl.multiple_of(n * width + (my_core + side) % NCORE * HEAD_DIM, HEAD_DIM)
            rows[:, pl.ds(column, HEAD_DIM)] = blocks[n * NCORE + side][...]
        chip = (my_x + NX - step) % NX
        total = total + jnp.dot(
            rows[:, n * width : (n + 1) * width],
            weight[pl.ds(pl.multiple_of(chip * width, width), width), :],
            preferred_element_type=F32,
        )
    sofar[...] = total
    for side in range(NCORE):
        late_weight[side * HEAD_DIM : (side + 1) * HEAD_DIM, :] = weight[weight_rows(LATE_STEP, side), :]


def project_rest(block, passed, sofar, weight, out, rows, staged, sems):
    rows[:, :HEAD_DIM] = block[...]
    rows[:, HEAD_DIM:] = passed[...]
    height = rows.shape[0] // OUT_CHUNKS
    copies = []
    for k in range(OUT_CHUNKS):
        some = pl.ds(k * height, height)
        total = sofar[some, :] + jnp.dot(rows[some, :], weight[...], preferred_element_type=F32)
        staged[some, :] = total.astype(BF16)
        copies.append(pltpu.make_async_copy(staged.at[some, :], out.at[some, :], sems.at[k]))
        copies[-1].start()
    for copy in copies:
        copy.wait()


def project_call(head, pairs, out_weight):
    early = [block for step in EARLY_STEPS for block in pairs[step]]
    tok_dev, out_width = early[0].shape[0], out_weight.shape[1]
    width = NCORE * HEAD_DIM
    sofar, late_weight = pl.pallas_call(
        project_most,
        name="project_most",
        in_specs=[SMEM] + [VMEM] * (len(early) + 1),
        out_specs=[VMEM] * 2,
        out_shape=[
            jax.ShapeDtypeStruct((tok_dev, out_width), F32),
            jax.ShapeDtypeStruct((width, out_width), BF16),
        ],
        scratch_shapes=[pltpu.VMEM((tok_dev, len(early) * HEAD_DIM), BF16)],
        compiler_params=PARAMS,
        cost_estimate=pl.CostEstimate(
            flops=2 * tok_dev * out_width * HEAD_DIM * len(early), bytes_accessed=4 << 20, transcendentals=0
        ),
    )(head, *early, out_weight)
    return pl.pallas_call(
        project_rest,
        name="project_rest",
        in_specs=[VMEM] * 4,
        out_specs=pl.BlockSpec(memory_space=pl.ANY),
        out_shape=jax.ShapeDtypeStruct((tok_dev, out_width), BF16),
        scratch_shapes=[
            pltpu.VMEM((tok_dev, width), BF16),
            pltpu.VMEM((tok_dev, out_width), BF16),
            pltpu.SemaphoreType.DMA((OUT_CHUNKS,)),
        ],
        compiler_params=PARAMS,
    )(*pairs[LATE_STEP], sofar, late_weight)


def shards(queries, keys_values, out_weight, group_owner, clip_ids, mask_types):
    tok_dev = queries.shape[0]
    rank = lax.axis_index("ctx").astype(jnp.int32).reshape(1)
    head = lax.axis_index("head").astype(jnp.int32).reshape(1)

    def onward(right, left):
        return lax.ppermute(right, "ctx", along_z(1)), lax.ppermute(left, "ctx", along_z(-1))

    right, left = onward(keys_values, keys_values)
    all_q = [lax.ppermute(queries, "ctx", along_y(-d)) for d in range(1, NY)]
    info = jnp.concatenate([rank, group_owner, clip_ids, mask_types])
    *own, own_q = pl.pallas_call(
        prepare,
        name="prepare",
        in_specs=[VMEM] * 2,
        out_specs=[VMEM] * 3,
        out_shape=[
            jax.ShapeDtypeStruct((PER_RANK, GROUP, HEAD_DIM), BF16),
            jax.ShapeDtypeStruct((PER_RANK, HEAD_DIM, GROUP), BF16),
            jax.ShapeDtypeStruct((PER_RANK, HEAD_DIM, GROUP), BF16),
        ],
        compiler_params=pltpu.CompilerParams(vmem_limit_bytes=8 << 20),
    )(keys_values, queries)
    others_q = pl.pallas_call(
        turn,
        name="turn",
        in_specs=[VMEM] * len(all_q),
        out_specs=VMEM,
        out_shape=jax.ShapeDtypeStruct((NQ - PER_RANK, HEAD_DIM, GROUP), BF16),
        compiler_params=pltpu.CompilerParams(vmem_limit_bytes=8 << 20),
        cost_estimate=pl.CostEstimate(flops=1 << 20, bytes_accessed=1 << 20, transcendentals=0),
    )(*all_q)
    all_q = [own_q, others_q]
    right, left, info, own = lax.optimization_barrier((right, left, info, own))

    next_right, next_left = onward(right, left)
    *state, q_turned = attend_call((0, -1, 1), EVERY, info, all_q, [own, (right,), (left,)], None, False)
    right, left, state = lax.optimization_barrier((next_right, next_left, state))

    next_right, next_left = onward(right, left)
    state = attend_call((-2, 2), EVERY, info, [q_turned], [(right,), (left,)], state, False)
    right, left, state = lax.optimization_barrier((next_right, next_left, state))

    far = onward(right[0], left[1])
    state = attend_call((-3, 3), EVERY, info, [q_turned], [(right,), (left,)], state, False)
    away = (2, 1, 3)
    *sent, acc, run_max, run_sum = attend_call((4,), away, info, [q_turned], [far], state, True)
    parts = [lax.ppermute(part, "ctx", along_y(d)) for d, part in zip(away, sent)]
    parts.append(attend_call((4,), (0,), info, [q_turned], [far], (acc, run_max, run_sum), True)[0])
    attended = pl.pallas_call(
        merge,
        name="merge",
        in_specs=[VMEM] * NY,
        out_specs=VMEM,
        out_shape=jax.ShapeDtypeStruct((tok_dev, HEAD_DIM), BF16),
        compiler_params=PARAMS,
    )(*parts)

    blocks = []
    for d in range(NX):
        block = attended if d == 0 else lax.ppermute(attended, "head", along_x(d))
        blocks.append([block, lax.ppermute(block, "head", other_core())])
    return project_call(head, blocks, out_weight)


def solution(mesh):
    placed = (P("ctx", "head"), P(None, "ctx", "head"), P(None, "head"), P(), P(), P())
    return jax.shard_map(
        shards, mesh=mesh, in_specs=placed, out_specs=P("ctx", "head"), check_vma=False
    )
```
